256 devices in a mesh: expert: 64 (over z, y, core), tensor: 4 (over x).
Axes of the slice: x: 4, y: 4, z: 8, core: 2. Of those that a mesh axis runs over, the one named last changes fastest.
Arguments:
- note_tokens: bfloat16 [32768, 2048], P(('expert', 'tensor')), may hold values from -6 to 6
- note_route: int32 [32768, 1], P(('expert', 'tensor')), may hold values from 0 to 63; in each aligned block of 128 rows (0 to 127, 128 to 255, ...) at most 4 rows name the same one
- note_prob: float32 [32768, 1], P(('expert', 'tensor')), may hold values from 0.3 to 1
- note_cotangent: bfloat16 [32768, 2048], P(('expert', 'tensor')), may hold values from -6 to 6
- small_gate: bfloat16 [2048, 65536], P(None, ('expert', 'tensor')), may hold values from -0.125 to 0.125
- small_up: bfloat16 [2048, 65536], P(None, ('expert', 'tensor')), may hold values from -0.125 to 0.125
- small_down: bfloat16 [65536, 2048], P(('expert', 'tensor')), may hold values from -0.1875 to 0.1875
- wide_tokens: bfloat16 [512, 2048], P(('expert', 'tensor')), may hold values from -6 to 6
- wide_prob: bfloat16 [512, 2], P(('expert', 'tensor')), may hold values from 0.19921875 to 1
- wide_cotangent: bfloat16 [512, 2048], P(('expert', 'tensor')), may hold values from -6 to 6
- wide_gate: bfloat16 [2048, 32768], P(None, ('expert', 'tensor')), may hold values from -0.125 to 0.125
- wide_up: bfloat16 [2048, 32768], P(None, ('expert', 'tensor')), may hold values from -0.125 to 0.125
- wide_down: bfloat16 [32768, 2048], P(('expert', 'tensor')), may hold values from -0.046875 to 0.046875
Outputs:
- note_output: bfloat16 [32768, 2048], P(('expert', 'tensor'))
- note_grad: bfloat16 [32768, 2048], P(('expert', 'tensor'))
- small_gate_grad: bfloat16 [2048, 65536], P(None, ('expert', 'tensor'))
- small_up_grad: bfloat16 [2048, 65536], P(None, ('expert', 'tensor'))
- small_down_grad: bfloat16 [65536, 2048], P(('expert', 'tensor'))
- wide_output: bfloat16 [512, 2048], P(('expert', 'tensor'))
- wide_grad: bfloat16 [512, 2048], P(('expert', 'tensor'))
- wide_gate_grad: bfloat16 [2048, 32768], P(None, ('expert', 'tensor'))
- wide_up_grad: bfloat16 [2048, 32768], P(None, ('expert', 'tensor'))
- wide_down_grad: bfloat16 [32768, 2048], P(('expert', 'tensor'))
The draws below stay inside these ranges and needn't reach their ends.
Inputs may be any that keep to these rules, and one draw needn't show every extreme that they name: `note_route`: in the rows of one device no small expert is named more than 4 times, a bound that some block reaches in some devices' rows.
All inputs are finite; a program needn't handle non-finite values.
Results may differ from the reference program's by a relative error of at most 0.0058.
Values may be sent and summed in bfloat16 or wider, within the bound.
No kernel may reach another device: no remote copies, remote signals or barrier semaphores. Data moves between devices by JAX's collectives and lax.ppermute only.
A program may use at most 128 MiB of HBM per device.

```python
import math
import jax
import jax.numpy as jnp
import numpy as np
from jax import lax

D = 2048
FFW = 16384
FFS = 1024
WIDE = 2
TOPK = 1
NOTE_DEV = 128
SMALL = 64
CAP = 4
NOTES = 32768
WIDES = 512
N_EXPERT = 64
N_TENSOR = 4


def level_of(key, extent, split, low, top_value):
    gain = 1.0
    for axis_at, blocks in split:
        heights = jax.random.uniform(jax.random.fold_in(jax.random.fold_in(key, 6), axis_at), (blocks,), jnp.float32, low / len(split), top_value / len(split))
        gain = gain * jnp.repeat(jnp.exp(heights), extent[axis_at] // blocks).reshape((-1,) + (1,) * (len(extent) - 1 - axis_at))
    return gain


def shared_out(key, own, number, rows, count, top, limit, slope):
    order = jax.random.permutation(key, count)
    packed, usual = portions_of(count, rows * top, limit, slope, True), portions_of(count, rows * top, limit, slope, False)
    places = jnp.arange(count)

    def named(tallies, rotation):
        used = int((tallies > 0).sum())
        fixed = max(1, used // 4)
        moved = fixed + (places - fixed + rotation * (used - fixed)) % max(1, count - fixed)
        return jnp.zeros((count,), jnp.int32).at[order[jnp.where(places < fixed, places, moved)]].set(jnp.asarray(tallies, jnp.int32))

    tallies = jnp.where(number % 4 == 0, named(packed, number // 4), named(usual, number - number // 4 - 1))
    mixed = jax.random.permutation(jax.random.fold_in(own, 3), count)
    giver, sink = mixed[0:count // 2 * 2:2], mixed[1:count // 2 * 2:2]
    slack = jnp.minimum(tallies[giver] - 1, limit - tallies[sink]) // 2
    slack = jnp.where((giver == order[0]) | (sink == order[0]) | (tallies[sink] == 0), 0, jnp.maximum(slack, 0))
    moved = jax.random.randint(jax.random.fold_in(own, 4), (count // 2,), 0, 1 << 20) % (slack + 1)
    tallies = tallies.at[giver].add(-moved).at[sink].add(moved)
    items = jnp.searchsorted(jnp.cumsum(tallies), jnp.arange(rows * top), side="right").astype(jnp.int32)
    grid = items.reshape(top, rows).T
    grid = grid[jax.random.permutation(jax.random.fold_in(own, 1), rows)]
    rotation = jax.random.randint(jax.random.fold_in(own, 2), (rows, 1), 0, top)
    return jnp.take_along_axis(grid, (jnp.arange(top)[None, :] + rotation) % top, axis=1)


def portions_of(count, total, reach, slope, full):
    weights = [(1 << 20) // math.isqrt(standing ** slope) + 1 for standing in range(1, count + 1)]
    largest = reach if full else min(reach, max(-(-total // count), total * weights[0] // sum(weights)))
    least = 1 if total - largest >= count - 1 else 0
    counts, surplus = [largest] + [least] * (count - 1), total - largest - least * (count - 1)
    while surplus > 0:
        free = [i for i in range(1, count) if counts[i] < largest] or [i for i in range(1, count) if counts[i] < reach]
        whole, left = sum([weights[i] for i in free]), surplus
        for i in free:
            more = min(reach - counts[i], max(1, left * weights[i] // whole), surplus)
            counts[i] = counts[i] + more
            surplus = surplus - more
    return np.array(counts)


def normal_values(rng, shape, scale, reach, split=(), held_as=jnp.bfloat16):
    array = scale * jax.random.normal(rng, shape, jnp.float32)
    if split:
        array = array * level_of(rng, shape, split, -0.22, 0.18)
    return jnp.clip(array, -reach, reach).astype(held_as)


def setup_inputs(seed: int = 0) -> dict:
    keys = jax.random.split(jax.random.key(seed), 14)
    note_tokens = normal_values(keys[0], (NOTES, D), 1.0, 6.0, ((0, 256),))
    note_route_keys = jax.random.split(jax.random.fold_in(keys[1], 1), NOTES // NOTE_DEV)
    note_route_turns = jax.random.permutation(jax.random.fold_in(keys[1], 3), NOTES // NOTE_DEV)
    note_route = jax.vmap(lambda own, number: shared_out(jax.random.fold_in(keys[1], 2), own, number, NOTE_DEV, SMALL, TOPK, CAP, 2))(note_route_keys, note_route_turns).reshape((NOTES, TOPK))
    note_prob = jnp.clip(0.3 + 0.7 * jax.random.uniform(keys[2], (NOTES, TOPK), jnp.float32) ** level_of(keys[2], (NOTES, TOPK), ((0, 256),), -0.2, 0.2), 0.3, 1.0)
    note_cotangent = normal_values(keys[3], (NOTES, D), 1.0, 6.0, ((0, 256),))
    small_gate = normal_values(keys[4], (D, SMALL * FFS), D ** -0.5, 0.125, ((1, 256),))
    small_up = normal_values(keys[5], (D, SMALL * FFS), D ** -0.5, 0.125, ((1, 256),))
    small_down = normal_values(keys[6], (SMALL * FFS, D), FFS ** -0.5, 0.1875, ((0, 256),))
    wide_tokens = normal_values(keys[7], (WIDES, D), 1.0, 6.0, ((0, 256),))
    wide_prob = jnp.clip(jnp.exp(math.log(1.0) - 1.6133518 * jax.random.uniform(keys[8], (WIDES, WIDE), jnp.float32) ** level_of(keys[8], (WIDES, WIDE), ((0, 256),), -0.2, 0.2)), 0.19921875, 1.0).astype(jnp.bfloat16)
    wide_cotangent = normal_values(keys[9], (WIDES, D), 1.0, 6.0, ((0, 256),))
    wide_gate = normal_values(keys[10], (D, WIDE * FFW), D ** -0.5, 0.125, ((1, 256),))
    wide_up = normal_values(keys[11], (D, WIDE * FFW), D ** -0.5, 0.125, ((1, 256),))
    wide_down = normal_values(keys[12], (WIDE * FFW, D), FFW ** -0.5, 0.046875, ((0, 256),))
    return dict(note_tokens=note_tokens, note_route=note_route, note_prob=note_prob, note_cotangent=note_cotangent, small_gate=small_gate, small_up=small_up, small_down=small_down, wide_tokens=wide_tokens, wide_prob=wide_prob, wide_cotangent=wide_cotangent, wide_gate=wide_gate, wide_up=wide_up, wide_down=wide_down)


def activation(gate_pre):
    sigma = jax.nn.sigmoid(gate_pre)
    return gate_pre * sigma, sigma * (1.0 + gate_pre * (1.0 - sigma))


def expert_step(row_block, cot_block, gate_weight, up_weight, down_weight):
    gate_pre = jnp.dot(row_block, gate_weight, preferred_element_type=jnp.float32)
    up_pre = jnp.dot(row_block, up_weight, preferred_element_type=jnp.float32)
    active, slope_term = activation(gate_pre)
    hidden = (active * up_pre).astype(jnp.bfloat16)
    slot_out = jnp.dot(hidden, down_weight, preferred_element_type=jnp.float32).astype(jnp.bfloat16)
    grad_hidden = jnp.dot(cot_block, down_weight.T, preferred_element_type=jnp.float32)
    grad_gate = (grad_hidden * up_pre * slope_term).astype(jnp.bfloat16)
    grad_up = (grad_hidden * active).astype(jnp.bfloat16)
    slot_grad = jnp.dot(grad_gate, gate_weight.T, preferred_element_type=jnp.float32)
    slot_grad = (slot_grad + jnp.dot(grad_up, up_weight.T, preferred_element_type=jnp.float32)).astype(jnp.bfloat16)
    gate_grad = jnp.dot(row_block.T, grad_gate, preferred_element_type=jnp.float32).astype(jnp.bfloat16)
    up_grad = jnp.dot(row_block.T, grad_up, preferred_element_type=jnp.float32).astype(jnp.bfloat16)
    down_grad = jnp.dot(hidden.T, cot_block, preferred_element_type=jnp.float32).astype(jnp.bfloat16)
    return slot_out, slot_grad, gate_grad, up_grad, down_grad


def reference(note_tokens, note_route, note_prob, note_cotangent, small_gate, small_up, small_down,
              wide_tokens, wide_prob, wide_cotangent, wide_gate, wide_up, wide_down):
    devices = N_EXPERT * N_TENSOR
    flat_route = note_route[:, 0].astype(jnp.int32)
    blocks = flat_route.reshape(devices, NOTE_DEV)
    labels = jnp.arange(SMALL, dtype=jnp.int32)
    onehot = (blocks[:, :, None] == labels[None, None, :]).astype(jnp.int32)
    rank_in = jnp.sum((jnp.cumsum(onehot, axis=1) - onehot) * onehot, axis=2)
    position = (jnp.arange(devices, dtype=jnp.int32)[:, None] * CAP + rank_in).reshape(-1).astype(jnp.int32)
    scaled = (note_prob[:, 0:1] * note_cotangent.astype(jnp.float32)).astype(jnp.bfloat16)
    rows_buf = jnp.zeros((SMALL, devices * CAP, D), jnp.bfloat16).at[flat_route, position].set(note_tokens)
    cots_buf = jnp.zeros((SMALL, devices * CAP, D), jnp.bfloat16).at[flat_route, position].set(scaled)
    gate_stack = small_gate.reshape(D, SMALL, FFS).transpose(1, 0, 2)
    up_stack = small_up.reshape(D, SMALL, FFS).transpose(1, 0, 2)
    down_stack = small_down.reshape(SMALL, FFS, D)
    out_buf, grad_buf, gate_parts, up_parts, down_parts = lax.map(
        lambda inputs: expert_step(*inputs), (rows_buf, cots_buf, gate_stack, up_stack, down_stack))
    note_output = (note_prob[:, 0:1] * out_buf[flat_route, position].astype(jnp.float32)).astype(jnp.bfloat16)
    note_grad = grad_buf[flat_route, position]
    small_gate_grad = gate_parts.transpose(1, 0, 2).reshape(D, SMALL * FFS)
    small_up_grad = up_parts.transpose(1, 0, 2).reshape(D, SMALL * FFS)
    small_down_grad = down_parts.reshape(SMALL * FFS, D)

    gate_probs = wide_prob.astype(jnp.float32)
    cotangent = wide_cotangent.astype(jnp.float32)
    total_out = jnp.zeros((WIDES, D), jnp.float32)
    total_grad = jnp.zeros((WIDES, D), jnp.float32)
    gate_list, up_list, down_list = [], [], []
    for member in range(WIDE):
        first = member * FFW
        gate_weight = wide_gate[:, first:first + FFW]
        up_weight = wide_up[:, first:first + FFW]
        down_weight = wide_down[first:first + FFW, :]
        gate_pre = jnp.dot(wide_tokens, gate_weight, preferred_element_type=jnp.float32)
        up_pre = jnp.dot(wide_tokens, up_weight, preferred_element_type=jnp.float32)
        active, slope_term = activation(gate_pre)
        hidden = (active * up_pre).astype(jnp.bfloat16)
        column = gate_probs[:, member:member + 1]
        total_out = total_out + column * jnp.dot(hidden, down_weight, preferred_element_type=jnp.float32)
        wide_scaled = (column * cotangent).astype(jnp.bfloat16)
        grad_hidden = jnp.dot(wide_scaled, down_weight.T, preferred_element_type=jnp.float32)
        grad_gate = (grad_hidden * up_pre * slope_term).astype(jnp.bfloat16)
        grad_up = (grad_hidden * active).astype(jnp.bfloat16)
        total_grad = total_grad + jnp.dot(grad_gate, gate_weight.T, preferred_element_type=jnp.float32)
        total_grad = total_grad + jnp.dot(grad_up, up_weight.T, preferred_element_type=jnp.float32)
        gate_list.append(jnp.dot(wide_tokens.T, grad_gate, preferred_element_type=jnp.float32).astype(jnp.bfloat16))
        up_list.append(jnp.dot(wide_tokens.T, grad_up, preferred_element_type=jnp.float32).astype(jnp.bfloat16))
        down_list.append(jnp.dot(hidden.T, wide_scaled, preferred_element_type=jnp.float32).astype(jnp.bfloat16))
    wide_output = total_out.astype(jnp.bfloat16)
    wide_grad = total_grad.astype(jnp.bfloat16)
    wide_gate_grad = jnp.concatenate(gate_list, axis=1)
    wide_up_grad = jnp.concatenate(up_list, axis=1)
    wide_down_grad = jnp.concatenate(down_list, axis=0)
    return (note_output, note_grad, small_gate_grad, small_up_grad, small_down_grad,
            wide_output, wide_grad, wide_gate_grad, wide_up_grad, wide_down_grad)
```

```python
import jax
import jax.numpy as jnp
from jax import lax
from jax.experimental import pallas as pl
from jax.experimental.pallas import tpu as pltpu
from jax.sharding import Mesh, PartitionSpec as P

F32 = jnp.float32
BF16 = jnp.bfloat16
EXPERT = ("z", "y", "core")
WHOLE = ("z", "y", "core", "x")


def activation(gate_pre):
    sigma = jax.nn.sigmoid(gate_pre)
    return (gate_pre * sigma, sigma * (1.0 + gate_pre * (1.0 - sigma)))


def mm(a, b):
    return jnp.dot(a, b, preferred_element_type=F32)


def mm_nt(a, b):
    return jnp.einsum("rh,dh->rd", a, b, preferred_element_type=F32)


def mm_tn(a, b):
    return jnp.einsum("rd,rh->dh", a, b, preferred_element_type=F32)


def slot_table(routing, experts, capacity):
    labels = jnp.arange(experts, dtype=jnp.int32)
    onehot = (routing[:, None] == labels[None, :]).astype(jnp.int32)
    earlier = jnp.cumsum(onehot, axis=0) - onehot
    rank_in = jnp.sum(earlier * onehot, axis=1)
    target = routing * capacity + rank_in
    places = jnp.arange(experts * capacity, dtype=jnp.int32)
    return (target[:, None] == places[None, :]).astype(BF16)


def pair_perm(flip):
    perm = []
    for core in range(2):
        for x in range(4):
            mate = x ^ 1 if core ^ flip == 0 else 3 - x
            perm.append((core * 4 + x, core * 4 + mate))
    return perm


ROW_PAIR = pair_perm(0)
WEIGHT_PAIR = pair_perm(1)


def row_swap(v):
    return lax.ppermute(v, ("core", "x"), ROW_PAIR)


def weight_swap(v):
    return lax.ppermute(v, ("core", "x"), WEIGHT_PAIR)


def shift(v, axis, by):
    n = lax.axis_size(axis)
    return lax.ppermute(v, axis, [(i, (i + by) % n) for i in range(n)])


def mirror(v, axis, bit):
    return lax.ppermute(v, axis, [(i, i ^ bit) for i in range(lax.axis_size(axis))])


def gather_x(v):
    return jnp.concatenate([v, shift(v, "x", 1), shift(v, "x", -1), shift(v, "x", 2)], axis=0)


def gather_near(v):
    half = v.shape[0] // 2
    below, above = shift(v, "y", 1), shift(v, "y", -1)
    far_a, far_b = shift(below[:half], "y", 1), shift(above[half:], "y", -1)
    pieces = [v, below, above, far_a, far_b]
    return pieces + [mirror(piece, "core", 1) for piece in pieces]


def collect_near(own, sent):
    v = own + mirror(sent, "core", 1).astype(F32)
    own, below, above, far = (v[i] for i in range(4))
    half = far.shape[0] // 2
    far = far.astype(BF16)
    from_a = shift(far[:half], "y", -1).astype(F32)
    from_b = shift(far[half:], "y", 1).astype(F32)
    below = jnp.concatenate([below[:half] + from_a, below[half:]], axis=0).astype(BF16)
    above = jnp.concatenate([above[:half], above[half:] + from_b], axis=0).astype(BF16)
    v = own + shift(below, "y", -1).astype(F32) + shift(above, "y", 1).astype(F32)
    rows = v.shape[0] // 4
    own, below, above, far = (v[i * rows : (i + 1) * rows] for i in range(4))
    v = own + shift(below.astype(BF16), "x", -1).astype(F32)
    v = v + shift(above.astype(BF16), "x", 1).astype(F32)
    return v + shift(far.astype(BF16), "x", 2).astype(F32)


def wide_kernel(*refs):
    pieces = refs[:10]
    place, gate, up, down, own_ref, sent_ref, dgate, dup, ddown = refs[10:19]
    rows, both, hidden, grads = refs[19:]
    width, units = gate.shape
    total, part = pieces[0].shape
    half = total // 2
    core, at_y = place[0], place[1]
    ys = [lax.rem(at_y + step, 4) for step in (0, 3, 1, 2)]
    for side in range(2):
        base = (core if side == 0 else 1 - core) * width
        spots = [pl.ds(pl.multiple_of(base + y * part, part), part) for y in ys]
        own, below, above, far_a, far_b = pieces[5 * side : 5 * side + 5]
        rows[:, spots[0]] = own[...]
        rows[:, spots[1]] = below[...]
        rows[:, spots[2]] = above[...]
        rows[:half, spots[3]] = far_a[...]
        rows[half:, spots[3]] = far_b[...]
    both[:, :units] = gate[...]
    both[:, units:] = up[...]
    chunk = 128

    @pl.loop(0, total // chunk)
    def _(i):
        here = pl.ds(pl.multiple_of(i * chunk, chunk), chunk)
        pre = mm(rows[here, :width], both[...])
        gate_pre, up_pre = pre[:, :units], pre[:, units:]
        active, slope = activation(gate_pre)
        hidden[here, :] = (active * up_pre).astype(BF16)
        back = nt(rows[here, width:], down[...])
        grads[here, :units] = (back * up_pre * slope).astype(BF16)
        grads[here, units:] = (back * active).astype(BF16)
        for j, y in enumerate(ys):
            spot = pl.ds(pl.multiple_of(y * part, part), part)
            out = mm(hidden[here, :], down[:, spot])
            grad = nt(grads[here, :], both[spot, :])
            own_ref[j, here, :] = jnp.where(core == 0, out, grad)
            sent_ref[j, here, :] = jnp.where(core == 0, grad, out).astype(BF16)

    block = 256

    @pl.loop(0, width // block)
    def _(i):
        here = pl.ds(pl.multiple_of(i * block, block), block)
        there = pl.ds(pl.multiple_of(width + i * block, block), block)
        term = tn(rows[:, here], grads[...])
        dgate[here, :] = term[:, :units].astype(BF16)
        dup[here, :] = term[:, units:].astype(BF16)
        ddown[:, here] = tn(hidden[...], rows[:, there]).astype(BF16)


def wide_compute(pieces, place, gate, up, down):
    width, units = gate.shape
    total, part = pieces[0].shape
    inside = pl.BlockSpec(memory_space=pltpu.VMEM)
    return pl.pallas_call(
        wide_kernel,
        out_shape=(
            jax.ShapeDtypeStruct((4, total, part), F32),
            jax.ShapeDtypeStruct((4, total, part), BF16),
            jax.ShapeDtypeStruct(gate.shape, BF16),
            jax.ShapeDtypeStruct(up.shape, BF16),
            jax.ShapeDtypeStruct(down.shape, BF16),
        ),
        in_specs=[inside] * 10 + [pl.BlockSpec(memory_space=pltpu.SMEM)] + [inside] * 3,
        out_specs=[inside] * 5,
        scratch_shapes=[
            pltpu.VMEM((total, 2 * width), BF16),
            pltpu.VMEM((width, 2 * units), BF16),
            pltpu.VMEM((total, units), BF16),
            pltpu.VMEM((total, 2 * units), BF16),
        ],
        compiler_params=pltpu.CompilerParams(vmem_limit_bytes=40 << 20),
        cost_estimate=pl.CostEstimate(
            flops=18 * total * width * units, bytes_accessed=16 << 20, transcendentals=total * units
        ),
    )(*pieces, place, gate, up, down)


def nt(a, b):
    return lax.dot_general(a, b, (((1,), (1,)), ((), ())), preferred_element_type=F32)


def tn(a, b):
    return lax.dot_general(a, b, (((0,), (0,)), ((), ())), preferred_element_type=F32)


def exchange(v):
    return lax.all_to_all(v, EXPERT, split_axis=0, concat_axis=0, tiled=True)


def per_device(
    note_tokens,
    note_route,
    note_prob,
    note_cotangent,
    small_gate,
    small_up,
    small_down,
    wide_tokens,
    wide_prob,
    wide_cotangent,
    wide_gate,
    wide_up,
    wide_down,
):
    width = note_tokens.shape[1]
    experts = lax.axis_size(EXPERT)
    capacity = max(2, 2 * note_tokens.shape[0] // experts)

    half = experts * capacity
    units = small_gate.shape[1]
    nz, ny, nc = (lax.axis_size(name) for name in EXPERT)
    members = wide_prob.shape[1]
    wide_rows = wide_tokens.shape[0]

    own_both = jnp.concatenate([small_gate, small_up], axis=1)

    table = slot_table(note_route[:, 0], experts, capacity)
    scaled_cot = (note_prob * note_cotangent.astype(F32)).astype(BF16)
    placed_rows = mm_tn(table, note_tokens).astype(BF16)
    placed_cots = mm_tn(table, scaled_cot).astype(BF16)

    part = 2 * width // (ny * nc)
    side = part * wide_rows // capacity
    scaled = wide_prob.astype(F32)[:, :, None] * wide_cotangent.astype(F32)[:, None, :]
    pair = jnp.stack(
        [jnp.broadcast_to(wide_tokens[:, None, :], scaled.shape), scaled.astype(BF16)], axis=2
    )
    pair = pair.reshape(wide_rows, members, nc, ny, part).transpose(1, 3, 2, 0, 4)
    pair = jnp.broadcast_to(pair[:, None], (members, nz // members) + pair.shape[1:])
    beside = pair.reshape(half, side)
    mate_both = weight_swap(own_both)
    mate_down = weight_swap(small_down)

    blocks = (experts, capacity, width)
    placed_cots = placed_cots.reshape(blocks)
    arrived = exchange(jnp.concatenate([placed_rows, beside], axis=1).reshape(experts, capacity, -1))
    arrived, placed_cots = lax.optimization_barrier((arrived, placed_cots))
    own_cots = exchange(placed_cots)
    arrived, mate_both = lax.optimization_barrier((arrived, mate_both))
    near = gather_x(arrived[:, :, width:].reshape(experts * wide_rows, part))
    own_rows = arrived[:, :, :width].reshape(half, width)
    own_rows, near = lax.optimization_barrier((own_rows, near))
    rows = jnp.concatenate([own_rows, row_swap(own_rows)], axis=0)

    wide_pieces = gather_near(near)
    boths, downs = (own_both, mate_both), (small_down, mate_down)
    hidden, terms, grads = [], [], []
    for w in range(2):
        pre = mm(rows, boths[w])
        gate_pre, up_pre = pre[:, :units], pre[:, units:]
        active, slope = activation(gate_pre)
        hidden.append((active * up_pre).astype(BF16))
        terms.append((up_pre, active, slope))

    def out_part(r):
        here = slice(r * half, (r + 1) * half)
        return mm(hidden[0][here], downs[0]) + mm(hidden[1][here], downs[1])

    sent_out, own_cots, wide_pieces = lax.optimization_barrier(
        (out_part(1).astype(BF16), own_cots, wide_pieces)
    )
    mate_out = row_swap(sent_out)
    place = jnp.stack([lax.axis_index("core"), lax.axis_index("y")]).astype(jnp.int32)
    wide_own, wide_sent, wide_gate_grad, wide_up_grad, wide_down_grad = wide_compute(
        wide_pieces, place, wide_gate, wide_up, wide_down
    )
    own_cots = own_cots.reshape(half, width)
    cots = jnp.concatenate([own_cots, row_swap(own_cots)], axis=0)
    slot_out = (out_part(0) + mate_out.astype(F32)).astype(BF16)
    back_out = exchange(slot_out.reshape(blocks))

    for w in range(2):
        up_pre, active, slope = terms[w]
        grad_hidden = mm_nt(cots, downs[w])
        grads.append(
            jnp.concatenate(
                [
                    (grad_hidden * up_pre * slope).astype(BF16),
                    (grad_hidden * active).astype(BF16),
                ],
                axis=1,
            )
        )

    def grad_part(r):
        here = slice(r * half, (r + 1) * half)
        return mm_nt(grads[0][here], boths[0]) + mm_nt(grads[1][here], boths[1])

    sent_grad = grad_part(1).astype(BF16)
    sent_grad, grads = lax.optimization_barrier((sent_grad, grads))
    mate_grad = row_swap(sent_grad)
    slot_grad = (grad_part(0) + mate_grad.astype(F32)).astype(BF16)

    sums = collect_near(wide_own, wide_sent).astype(BF16).reshape(half, side)
    hidden, grads, sums, back_out = lax.optimization_barrier((hidden, grads, sums, back_out))
    back_all = exchange(jnp.concatenate([slot_grad, sums], axis=1).reshape(experts, capacity, -1))
    back_all = back_all.reshape(half, width + side)
    back_grad = back_all[:, :width]
    sums = back_all[:, width:].astype(F32).reshape(members, nz // members, ny, nc, wide_rows, part)
    sums = jnp.sum(sums, axis=1).transpose(0, 2, 3, 1, 4).reshape(members, nc, wide_rows, width)
    weights = wide_prob.astype(F32).T[:, :, None]
    wide_output = jnp.sum(sums[:, 0] * weights, axis=0).astype(BF16)
    wide_grad = jnp.sum(sums[:, 1], axis=0).astype(BF16)

    both_sent = weight_swap(mm_tn(rows, grads[1]).astype(BF16))
    down_sent = weight_swap(mm_tn(hidden[1], cots).astype(BF16))
    both_grad = (mm_tn(rows, grads[0]) + both_sent.astype(F32)).astype(BF16)
    small_gate_grad, small_up_grad = both_grad[:, :units], both_grad[:, units:]
    small_down_grad = (mm_tn(hidden[0], cots) + down_sent.astype(F32)).astype(BF16)

    note_output = (note_prob * mm(table, back_out.reshape(half, width))).astype(BF16)
    note_grad = mm(table, back_grad).astype(BF16)
    return (
        note_output,
        note_grad,
        small_gate_grad,
        small_up_grad,
        small_down_grad,
        wide_output,
        wide_grad,
        wide_gate_grad,
        wide_up_grad,
        wide_down_grad,
    )


def solution(mesh):
    grid = Mesh(mesh.devices.reshape(8, 4, 2, 4), WHOLE)
    rows = P(WHOLE, None)
    columns = P(None, WHOLE)
    return jax.shard_map(
        per_device,
        mesh=grid,
        in_specs=(
            rows, rows, rows, rows, columns, columns, rows, rows, rows, rows, columns, columns, rows,
        ),
        out_specs=(rows, rows, columns, columns, rows, rows, rows, columns, columns, rows),
        check_vma=False,
    )
```

```python
import jax
import jax.numpy as jnp
from jax import lax
from jax.experimental import pallas as pl
from jax.experimental.pallas import tpu as pltpu
from jax.sharding import Mesh, PartitionSpec as P

F32 = jnp.float32
BF16 = jnp.bfloat16
EXPERT = ("z", "y", "core")
WHOLE = ("z", "y", "core", "x")


def activation(gate_pre):
    sigma = jax.nn.sigmoid(gate_pre)
    return (gate_pre * sigma, sigma * (1.0 + gate_pre * (1.0 - sigma)))


def mm(a, b):
    return jnp.dot(a, b, preferred_element_type=F32)


def mm_nt(a, b):
    return jnp.einsum("rh,dh->rd", a, b, preferred_element_type=F32)


def mm_tn(a, b):
    return jnp.einsum("rd,rh->dh", a, b, preferred_element_type=F32)


def slot_rank(routing, experts, capacity):
    labels = jnp.arange(experts, dtype=jnp.int32)
    onehot = (routing[:, None] == labels[None, :]).astype(jnp.int32)
    earlier = jnp.cumsum(onehot, axis=0) - onehot
    return jnp.sum(earlier * onehot, axis=1)


def places(at, count):
    return (at[:, None] == jnp.arange(count, dtype=jnp.int32)[None, :]).astype(BF16)


def pair_perm(flip):
    perm = []
    for core in range(2):
        for x in range(4):
            mate = x ^ 1 if core ^ flip == 0 else 3 - x
            perm.append((core * 4 + x, core * 4 + mate))
    return perm


ROW_PAIR = pair_perm(0)
WEIGHT_PAIR = pair_perm(1)


def row_swap(v):
    return lax.ppermute(v, ("core", "x"), ROW_PAIR)


def weight_swap(v):
    return lax.ppermute(v, ("core", "x"), WEIGHT_PAIR)


def shift(v, axis, by):
    n = lax.axis_size(axis)
    return lax.ppermute(v, axis, [(i, (i + by) % n) for i in range(n)])


def mirror(v, axis, bit):
    return lax.ppermute(v, axis, [(i, i ^ bit) for i in range(lax.axis_size(axis))])


def gather_x(v):
    return jnp.concatenate([v, shift(v, "x", 1), shift(v, "x", -1), shift(v, "x", 2)], axis=0)


def gather_near(v):
    half = v.shape[0] // 2
    below, above = shift(v, "y", 1), shift(v, "y", -1)
    far_a, far_b = shift(below[:half], "y", 1), shift(above[half:], "y", -1)
    pieces = [v, below, above, far_a, far_b]
    return pieces + [mirror(piece, "core", 1) for piece in pieces]


def collect_near(own, sent):
    v = own + mirror(sent, "core", 1).astype(F32)
    own, below, above, far = (v[i] for i in range(4))
    half = far.shape[0] // 2
    far = far.astype(BF16)
    from_a = shift(far[:half], "y", -1).astype(F32)
    from_b = shift(far[half:], "y", 1).astype(F32)
    below = jnp.concatenate([below[:half] + from_a, below[half:]], axis=0).astype(BF16)
    above = jnp.concatenate([above[:half], above[half:] + from_b], axis=0).astype(BF16)
    v = own + shift(below, "y", -1).astype(F32) + shift(above, "y", 1).astype(F32)
    rows = v.shape[0] // 4
    own, below, above, far = (v[i * rows : (i + 1) * rows] for i in range(4))
    v = own + shift(below.astype(BF16), "x", -1).astype(F32)
    v = v + shift(above.astype(BF16), "x", 1).astype(F32)
    return v + shift(far.astype(BF16), "x", 2).astype(F32)


def wide_kernel(*refs):
    pieces = refs[:10]
    place, gate, up, down, own_ref, sent_ref, dgate, dup, ddown = refs[11:20]
    rows, both, hidden, grads = refs[20:]
    width, units = gate.shape
    total, part = pieces[0].shape
    half = total // 2
    core, at_y = place[0], place[1]
    ys = [lax.rem(at_y + step, 4) for step in (0, 3, 1, 2)]
    for side in range(2):
        base = (core if side == 0 else 1 - core) * width
        spots = [pl.ds(pl.multiple_of(base + y * part, part), part) for y in ys]
        own, below, above, far_a, far_b = pieces[5 * side : 5 * side + 5]
        rows[:, spots[0]] = own[...]
        rows[:, spots[1]] = below[...]
        rows[:, spots[2]] = above[...]
        rows[:half, spots[3]] = far_a[...]
        rows[half:, spots[3]] = far_b[...]
    both[:, :units] = gate[...]
    both[:, units:] = up[...]
    chunk = 128

    @pl.loop(0, total // chunk)
    def _(i):
        here = pl.ds(pl.multiple_of(i * chunk, chunk), chunk)
        pre = mm(rows[here, :width], both[...])
        gate_pre, up_pre = pre[:, :units], pre[:, units:]
        active, slope = activation(gate_pre)
        hidden[here, :] = (active * up_pre).astype(BF16)
        back = nt(rows[here, width:], down[...])
        grads[here, :units] = (back * up_pre * slope).astype(BF16)
        grads[here, units:] = (back * active).astype(BF16)
        for j, y in enumerate(ys):
            spot = pl.ds(pl.multiple_of(y * part, part), part)
            out = mm(hidden[here, :], down[:, spot])
            grad = nt(grads[here, :], both[spot, :])
            own_ref[j, here, :] = jnp.where(core == 0, out, grad)
            sent_ref[j, here, :] = jnp.where(core == 0, grad, out).astype(BF16)

    block = 256

    @pl.loop(0, width // block)
    def _(i):
        here = pl.ds(pl.multiple_of(i * block, block), block)
        there = pl.ds(pl.multiple_of(width + i * block, block), block)
        term = tn(rows[:, here], grads[...])
        dgate[here, :] = term[:, :units].astype(BF16)
        dup[here, :] = term[:, units:].astype(BF16)
        ddown[:, here] = tn(hidden[...], rows[:, there]).astype(BF16)


def wide_compute(pieces, after, place, gate, up, down):
    width, units = gate.shape
    total, part = pieces[0].shape
    inside = pl.BlockSpec(memory_space=pltpu.VMEM)
    return pl.pallas_call(
        wide_kernel,
        out_shape=(
            jax.ShapeDtypeStruct((4, total, part), F32),
            jax.ShapeDtypeStruct((4, total, part), BF16),
            jax.ShapeDtypeStruct(gate.shape, BF16),
            jax.ShapeDtypeStruct(up.shape, BF16),
            jax.ShapeDtypeStruct(down.shape, BF16),
        ),
        in_specs=[inside] * 11 + [pl.BlockSpec(memory_space=pltpu.SMEM)] + [inside] * 3,
        out_specs=[inside] * 5,
        scratch_shapes=[
            pltpu.VMEM((total, 2 * width), BF16),
            pltpu.VMEM((width, 2 * units), BF16),
            pltpu.VMEM((total, units), BF16),
            pltpu.VMEM((total, 2 * units), BF16),
        ],
        compiler_params=pltpu.CompilerParams(vmem_limit_bytes=40 << 20),
        cost_estimate=pl.CostEstimate(
            flops=18 * total * width * units, bytes_accessed=16 << 20, transcendentals=total * units
        ),
    )(*pieces, after, place, gate, up, down)


def nt(a, b):
    return lax.dot_general(a, b, (((1,), (1,)), ((), ())), preferred_element_type=F32)


def tn(a, b):
    return lax.dot_general(a, b, (((0,), (0,)), ((), ())), preferred_element_type=F32)


def exchange(v):
    return lax.all_to_all(v, EXPERT, split_axis=0, concat_axis=0, tiled=True)


def per_device(
    note_tokens,
    note_route,
    note_prob,
    note_cotangent,
    small_gate,
    small_up,
    small_down,
    wide_tokens,
    wide_prob,
    wide_cotangent,
    wide_gate,
    wide_up,
    wide_down,
):
    width = note_tokens.shape[1]
    experts = lax.axis_size(EXPERT)
    capacity = max(2, 2 * note_tokens.shape[0] // experts)

    half = experts * capacity
    units = small_gate.shape[1]
    nz, ny, nc = (lax.axis_size(name) for name in EXPERT)
    members = wide_prob.shape[1]
    wide_rows = wide_tokens.shape[0]

    own_both = jnp.concatenate([small_gate, small_up], axis=1)

    part = 2 * width // (ny * nc)
    scaled = wide_prob.astype(F32)[:, :, None] * wide_cotangent.astype(F32)[:, None, :]
    pair = jnp.stack(
        [jnp.broadcast_to(wide_tokens[:, None, :], scaled.shape), scaled.astype(BF16)], axis=2
    )
    pair = pair.reshape(wide_rows, members, nc, ny, part).transpose(1, 3, 2, 0, 4)
    pair = jnp.broadcast_to(pair[:, None], (members, nz // members) + pair.shape[1:])
    near = exchange(pair.reshape(experts, wide_rows, part)).reshape(experts * wide_rows, part)

    routing = note_route[:, 0]
    rank = slot_rank(routing, experts, capacity)
    table = places(routing * capacity + rank, half)
    first = 2 * routing * capacity + rank
    row_table, cot_table = places(first, 2 * half), places(first + capacity, 2 * half)
    scaled_cot = (note_prob * note_cotangent.astype(F32)).astype(BF16)
    placed = mm_tn(
        jnp.concatenate([row_table, cot_table], axis=0),
        jnp.concatenate([note_tokens, scaled_cot], axis=0),
    ).astype(BF16)
    placed, near = lax.optimization_barrier((placed, near))
    arrived = exchange(placed.reshape(experts, 2 * capacity, width))

    near = gather_x(near)
    near, own_both, small_down = lax.optimization_barrier((near, own_both, small_down))
    mate_both = weight_swap(own_both)
    mate_down = weight_swap(small_down)
    arrived, mate_both, mate_down = lax.optimization_barrier((arrived, mate_both, mate_down))
    own_rows = arrived[:, :capacity].reshape(half, width)
    own_cots = arrived[:, capacity:].reshape(half, width)
    rows = jnp.concatenate([own_rows, row_swap(own_rows)], axis=0)
    mate_cots = row_swap(own_cots)

    wide_pieces = gather_near(near)
    place = jnp.stack([lax.axis_index("core"), lax.axis_index("y")]).astype(jnp.int32)
    wide_own, wide_sent, wide_gate_grad, wide_up_grad, wide_down_grad = wide_compute(
        wide_pieces, own_cots[:16, :128], place, wide_gate, wide_up, wide_down
    )


    boths, downs = (own_both, mate_both), (small_down, mate_down)
    blocks = (experts, capacity, width)
    hidden, terms, grads = [], [], []
    for w in range(2):
        pre = mm(rows, boths[w])
        gate_pre, up_pre = pre[:, :units], pre[:, units:]
        active, slope = activation(gate_pre)
        hidden.append((active * up_pre).astype(BF16))
        terms.append((up_pre, active, slope))

    def out_part(r):
        here = slice(r * half, (r + 1) * half)
        return mm(hidden[0][here], downs[0]) + mm(hidden[1][here], downs[1])

    sent_out, own_out, mate_cots = lax.optimization_barrier(
        (out_part(1).astype(BF16), out_part(0), mate_cots)
    )
    slot_out = (own_out + row_swap(sent_out).astype(F32)).astype(BF16)
    back_out = exchange(slot_out.reshape(blocks)).reshape(half, width)

    cots = jnp.concatenate([own_cots, mate_cots], axis=0)
    for w in range(2):
        up_pre, active, slope = terms[w]
        grad_hidden = mm_nt(cots, downs[w])
        grads.append(
            jnp.concatenate(
                [
                    (grad_hidden * up_pre * slope).astype(BF16),
                    (grad_hidden * active).astype(BF16),
                ],
                axis=1,
            )
        )

    def grad_part(r):
        here = slice(r * half, (r + 1) * half)
        return mm_nt(grads[0][here], boths[0]) + mm_nt(grads[1][here], boths[1])

    mate_grad = row_swap(grad_part(1).astype(BF16))

    def both_term(w):
        return mm_tn(rows, grads[w])

    def down_term(w):
        return mm_tn(hidden[w], cots)

    side = part * wide_rows // capacity
    sums = collect_near(wide_own, wide_sent).astype(BF16).reshape(half, side)
    both_sent, down_sent, sums, own_grad, back_out = lax.optimization_barrier(
        (both_term(1).astype(BF16), down_term(1).astype(BF16), sums, grad_part(0), back_out)
    )
    slot_grad = (own_grad + mate_grad.astype(F32)).astype(BF16)
    back = jnp.concatenate([slot_grad, sums], axis=1).reshape(experts, capacity, -1)
    back = exchange(back).reshape(half, width + side)
    sums = back[:, width:].astype(F32).reshape(members, nz // members, ny, nc, wide_rows, part)
    sums = jnp.sum(sums, axis=1).transpose(0, 2, 3, 1, 4).reshape(members, nc, wide_rows, width)
    weights = wide_prob.astype(F32).T[:, :, None]
    wide_output = jnp.sum(sums[:, 0] * weights, axis=0).astype(BF16)
    wide_grad = jnp.sum(sums[:, 1], axis=0).astype(BF16)

    both_grad = (both_term(0) + weight_swap(both_sent).astype(F32)).astype(BF16)
    small_gate_grad, small_up_grad = both_grad[:, :units], both_grad[:, units:]
    small_down_grad = (down_term(0) + weight_swap(down_sent).astype(F32)).astype(BF16)

    note_output = (note_prob * mm(table, back_out)).astype(BF16)
    note_grad = mm(table, back[:, :width]).astype(BF16)
    return (
        note_output,
        note_grad,
        small_gate_grad,
        small_up_grad,
        small_down_grad,
        wide_output,
        wide_grad,
        wide_gate_grad,
        wide_up_grad,
        wide_down_grad,
    )


def solution(mesh):
    grid = Mesh(mesh.devices.reshape(8, 4, 2, 4), WHOLE)
    rows = P(WHOLE, None)
    columns = P(None, WHOLE)
    return jax.shard_map(
        per_device,
        mesh=grid,
        in_specs=(
            rows, rows, rows, rows, columns, columns, rows, rows, rows, rows, columns, columns, rows,
        ),
        out_specs=(rows, rows, columns, columns, rows, rows, rows, columns, columns, rows),
        check_vma=False,
    )
```

```python
import jax
import jax.numpy as jnp
from jax import lax
from jax.experimental import pallas as pl
from jax.experimental.pallas import tpu as pltpu
from jax.sharding import Mesh, PartitionSpec as P

F32 = jnp.float32
BF16 = jnp.bfloat16
EXPERT = ("z", "y", "core")
WHOLE = ("z", "y", "core", "x")


def activation(gate_pre):
    sigma = jax.nn.sigmoid(gate_pre)
    return (gate_pre * sigma, sigma * (1.0 + gate_pre * (1.0 - sigma)))


def mm(a, b):
    return jnp.dot(a, b, preferred_element_type=F32)


def mm_nt(a, b):
    return jnp.einsum("rh,dh->rd", a, b, preferred_element_type=F32)


def mm_tn(a, b):
    return jnp.einsum("rd,rh->dh", a, b, preferred_element_type=F32)


def slot_rank(routing, experts, capacity):
    labels = jnp.arange(experts, dtype=jnp.int32)
    onehot = (routing[:, None] == labels[None, :]).astype(jnp.int32)
    earlier = jnp.cumsum(onehot, axis=0) - onehot
    return jnp.sum(earlier * onehot, axis=1)


def places(at, count):
    return (at[:, None] == jnp.arange(count, dtype=jnp.int32)[None, :]).astype(BF16)


def pair_perm(flip):
    perm = []
    for core in range(2):
        for x in range(4):
            mate = x ^ 1 if core ^ flip == 0 else 3 - x
            perm.append((core * 4 + x, core * 4 + mate))
    return perm


ROW_PAIR = pair_perm(0)
WEIGHT_PAIR = pair_perm(1)


def row_swap(v):
    return lax.ppermute(v, ("core", "x"), ROW_PAIR)


def weight_swap(v):
    return lax.ppermute(v, ("core", "x"), WEIGHT_PAIR)


def shift(v, axis, by):
    n = lax.axis_size(axis)
    return lax.ppermute(v, axis, [(i, (i + by) % n) for i in range(n)])


def mirror(v, axis, bit):
    return lax.ppermute(v, axis, [(i, i ^ bit) for i in range(lax.axis_size(axis))])


def gather_x(v):
    return jnp.concatenate([v, shift(v, "x", 1), shift(v, "x", -1), shift(v, "x", 2)], axis=0)


def gather_near(v):
    half = v.shape[0] // 2
    below, above = shift(v, "y", 1), shift(v, "y", -1)
    far_a, far_b = shift(below[:half], "y", 1), shift(above[half:], "y", -1)
    return [v, below, above, far_a, far_b]


def collect_far(own, sent):
    v = own + mirror(sent, "core", 1).astype(F32)
    half = v.shape[1] // 2
    far = v[3].astype(BF16)
    return v, shift(far[:half], "y", -1), shift(far[half:], "y", 1)


def collect_turn(v, from_a, from_b):
    below, above = v[1], v[2]
    half = below.shape[0] // 2
    from_a, from_b = from_a.astype(F32), from_b.astype(F32)
    below = jnp.concatenate([below[:half] + from_a, below[half:]], axis=0).astype(BF16)
    above = jnp.concatenate([above[:half], above[half:] + from_b], axis=0).astype(BF16)
    return below, above


def collect_near(v, below, above):
    return v[0] + shift(below, "y", -1).astype(F32) + shift(above, "y", 1).astype(F32)


def collect_x(v):
    rows = v.shape[0] // 4
    own, below, above, far = (v[i * rows : (i + 1) * rows] for i in range(4))
    v = own + shift(below.astype(BF16), "x", -1).astype(F32)
    v = v + shift(above.astype(BF16), "x", 1).astype(F32)
    return v + shift(far.astype(BF16), "x", 2).astype(F32)


def wide_kernel(*refs):
    pieces = refs[:10]
    place, gate, up, down, own_ref, sent_ref, dgate, dup, ddown = refs[11:20]
    rows, both, hidden, grads = refs[20:]
    width, units = gate.shape
    total, part = pieces[0].shape
    half = total // 2
    core, at_y = place[0], place[1]
    ys = [lax.rem(at_y + step, 4) for step in (0, 3, 1, 2)]
    for side in range(2):
        base = (core if side == 0 else 1 - core) * width
        spots = [pl.ds(pl.multiple_of(base + y * part, part), part) for y in ys]
        own, below, above, far_a, far_b = pieces[5 * side : 5 * side + 5]
        rows[:, spots[0]] = own[...]
        rows[:, spots[1]] = below[...]
        rows[:, spots[2]] = above[...]
        rows[:half, spots[3]] = far_a[...]
        rows[half:, spots[3]] = far_b[...]
    both[:, :units] = gate[...]
    both[:, units:] = up[...]
    chunk = 128

    @pl.loop(0, total // chunk)
    def _(i):
        here = pl.ds(pl.multiple_of(i * chunk, chunk), chunk)
        pre = mm(rows[here, :width], both[...])
        gate_pre, up_pre = pre[:, :units], pre[:, units:]
        active, slope = activation(gate_pre)
        hidden[here, :] = (active * up_pre).astype(BF16)
        back = nt(rows[here, width:], down[...])
        grads[here, :units] = (back * up_pre * slope).astype(BF16)
        grads[here, units:] = (back * active).astype(BF16)
        for j, y in enumerate(ys):
            spot = pl.ds(pl.multiple_of(y * part, part), part)
            out = mm(hidden[here, :], down[:, spot])
            grad = nt(grads[here, :], both[spot, :])
            own_ref[j, here, :] = jnp.where(core == 0, out, grad)
            sent_ref[j, here, :] = jnp.where(core == 0, grad, out).astype(BF16)

    block = 256

    @pl.loop(0, width // block)
    def _(i):
        here = pl.ds(pl.multiple_of(i * block, block), block)
        there = pl.ds(pl.multiple_of(width + i * block, block), block)
        term = tn(rows[:, here], grads[...])
        dgate[here, :] = term[:, :units].astype(BF16)
        dup[here, :] = term[:, units:].astype(BF16)
        ddown[:, here] = tn(hidden[...], rows[:, there]).astype(BF16)


def wide_compute(pieces, after, place, gate, up, down):
    width, units = gate.shape
    total, part = pieces[0].shape
    inside = pl.BlockSpec(memory_space=pltpu.VMEM)
    return pl.pallas_call(
        wide_kernel,
        out_shape=(
            jax.ShapeDtypeStruct((4, total, part), F32),
            jax.ShapeDtypeStruct((4, total, part), BF16),
            jax.ShapeDtypeStruct(gate.shape, BF16),
            jax.ShapeDtypeStruct(up.shape, BF16),
            jax.ShapeDtypeStruct(down.shape, BF16),
        ),
        in_specs=[inside] * 11 + [pl.BlockSpec(memory_space=pltpu.SMEM)] + [inside] * 3,
        out_specs=[inside] * 5,
        scratch_shapes=[
            pltpu.VMEM((total, 2 * width), BF16),
            pltpu.VMEM((width, 2 * units), BF16),
            pltpu.VMEM((total, units), BF16),
            pltpu.VMEM((total, 2 * units), BF16),
        ],
        compiler_params=pltpu.CompilerParams(vmem_limit_bytes=40 << 20),
        cost_estimate=pl.CostEstimate(
            flops=18 * total * width * units, bytes_accessed=16 << 20, transcendentals=total * units
        ),
    )(*pieces, after, place, gate, up, down)


def nt(a, b):
    return lax.dot_general(a, b, (((1,), (1,)), ((), ())), preferred_element_type=F32)


def tn(a, b):
    return lax.dot_general(a, b, (((0,), (0,)), ((), ())), preferred_element_type=F32)


def exchange(v):
    return lax.all_to_all(v, EXPERT, split_axis=0, concat_axis=0, tiled=True)


def per_device(
    note_tokens,
    note_route,
    note_prob,
    note_cotangent,
    small_gate,
    small_up,
    small_down,
    wide_tokens,
    wide_prob,
    wide_cotangent,
    wide_gate,
    wide_up,
    wide_down,
):
    width = note_tokens.shape[1]
    experts = lax.axis_size(EXPERT)
    capacity = max(2, 2 * note_tokens.shape[0] // experts)

    half = experts * capacity
    units = small_gate.shape[1]
    nz, ny, nc = (lax.axis_size(name) for name in EXPERT)
    members = wide_prob.shape[1]
    wide_rows = wide_tokens.shape[0]

    own_both = jnp.concatenate([small_gate, small_up], axis=1)

    part = 2 * width // (ny * nc)
    scaled = wide_prob.astype(F32)[:, :, None] * wide_cotangent.astype(F32)[:, None, :]
    pair = jnp.stack(
        [jnp.broadcast_to(wide_tokens[:, None, :], scaled.shape), scaled.astype(BF16)], axis=2
    )
    pair = pair.reshape(wide_rows, members, nc, ny, part).transpose(1, 3, 2, 0, 4)
    pair = jnp.broadcast_to(pair[:, None], (members, nz // members) + pair.shape[1:])
    near = exchange(pair.reshape(experts, wide_rows, part)).reshape(experts * wide_rows, part)

    routing = note_route[:, 0]
    rank = slot_rank(routing, experts, capacity)
    table = places(routing * capacity + rank, half)
    first = 2 * routing * capacity + rank
    row_table, cot_table = places(first, 2 * half), places(first + capacity, 2 * half)
    scaled_cot = (note_prob * note_cotangent.astype(F32)).astype(BF16)
    placed = mm_tn(
        jnp.concatenate([row_table, cot_table], axis=0),
        jnp.concatenate([note_tokens, scaled_cot], axis=0),
    ).astype(BF16)
    placed, near = lax.optimization_barrier((placed, near))
    arrived = exchange(placed.reshape(experts, 2 * capacity, width))

    near = gather_x(near)
    near, own_both, small_down = lax.optimization_barrier((near, own_both, small_down))
    mate_both = weight_swap(own_both)
    mate_down = weight_swap(small_down)
    wide_pieces = gather_near(near)
    *near_pieces, far_a, far_b = wide_pieces
    arrived, mate_both, mate_down, far_a, far_b = lax.optimization_barrier(
        (arrived, mate_both, mate_down, far_a, far_b)
    )
    wide_pieces = near_pieces + [far_a, far_b]
    wide_pieces = wide_pieces + [mirror(piece, "core", 1) for piece in wide_pieces]
    slot = jnp.arange(2 * half, dtype=jnp.int32)
    order = slot % half // capacity * 2 * capacity + slot // half * capacity + slot % capacity
    sorted_slots = mm(places(order, 2 * half), arrived.reshape(2 * half, width)).astype(BF16)
    own_rows, own_cots = sorted_slots[:half], sorted_slots[half:]
    rows = lax.optimization_barrier(jnp.concatenate([own_rows, row_swap(own_rows)], axis=0))
    mate_cots = row_swap(own_cots)

    place = jnp.stack([lax.axis_index("core"), lax.axis_index("y")]).astype(jnp.int32)
    wide_own, wide_sent, wide_gate_grad, wide_up_grad, wide_down_grad = wide_compute(
        wide_pieces, own_rows[:16, :128], place, wide_gate, wide_up, wide_down
    )


    boths, downs = (own_both, mate_both), (small_down, mate_down)
    blocks = (experts, capacity, width)
    hidden, terms, grads = [], [], []
    for w in range(2):
        pre = mm(rows, boths[w])
        gate_pre, up_pre = pre[:, :units], pre[:, units:]
        active, slope = activation(gate_pre)
        hidden.append((active * up_pre).astype(BF16))
        terms.append((up_pre, active, slope))

    def out_part(r):
        here = slice(r * half, (r + 1) * half)
        return mm(hidden[0][here], downs[0]) + mm(hidden[1][here], downs[1])

    sent_out, own_out, mate_cots = lax.optimization_barrier(
        (out_part(1).astype(BF16), out_part(0), mate_cots)
    )
    mate_out = row_swap(sent_out)
    wide_part, from_a, from_b = collect_far(wide_own, wide_sent)
    below, above = collect_turn(wide_part, from_a, from_b)
    mate_out, mate_cots, below, above = lax.optimization_barrier(
        (mate_out, mate_cots, below, above)
    )
    slot_out, mate_cots = lax.optimization_barrier(
        ((own_out + mate_out.astype(F32)).astype(BF16), mate_cots)
    )
    back_out = exchange(slot_out.reshape(blocks)).reshape(half, width)
    cots = jnp.concatenate([own_cots, mate_cots], axis=0)
    for w in range(2):
        up_pre, active, slope = terms[w]
        grad_hidden = mm_nt(cots, downs[w])
        grads.append(
            jnp.concatenate(
                [
                    (grad_hidden * up_pre * slope).astype(BF16),
                    (grad_hidden * active).astype(BF16),
                ],
                axis=1,
            )
        )

    def grad_part(r):
        here = slice(r * half, (r + 1) * half)
        return mm_nt(grads[0][here], boths[0]) + mm_nt(grads[1][here], boths[1])

    mate_grad = row_swap(grad_part(1).astype(BF16))

    def both_term(w):
        return mm_tn(rows, grads[w])

    def down_term(w):
        return mm_tn(hidden[w], cots)

    side = part * wide_rows // capacity
    wide_part, both_sent = lax.optimization_barrier(
        (collect_near(wide_part, below, above), both_term(1).astype(BF16))
    )
    sums = collect_x(wide_part).astype(BF16).reshape(half, side)
    down_mate = weight_swap(down_term(1).astype(BF16))
    both_sent, down_mate, sums, own_grad, back_out = lax.optimization_barrier(
        (both_sent, down_mate, sums, grad_part(0), back_out)
    )
    slot_grad = (own_grad + mate_grad.astype(F32)).astype(BF16)
    back = jnp.concatenate([slot_grad, sums], axis=1).reshape(experts, capacity, -1)
    back = exchange(back).reshape(half, width + side)
    sums = back[:, width:].astype(F32).reshape(members, nz // members, ny, nc, wide_rows, part)
    sums = jnp.sum(sums, axis=1).transpose(0, 2, 3, 1, 4).reshape(members, nc, wide_rows, width)
    weights = wide_prob.astype(F32).T[:, :, None]
    wide_output = jnp.sum(sums[:, 0] * weights, axis=0).astype(BF16)
    wide_grad = jnp.sum(sums[:, 1], axis=0).astype(BF16)

    both_grad = (both_term(0) + weight_swap(both_sent).astype(F32)).astype(BF16)
    small_gate_grad, small_up_grad = both_grad[:, :units], both_grad[:, units:]
    small_down_grad = (down_term(0) + down_mate.astype(F32)).astype(BF16)

    note_output = (note_prob * mm(table, back_out)).astype(BF16)
    note_grad = mm(table, back[:, :width]).astype(BF16)
    return (
        note_output,
        note_grad,
        small_gate_grad,
        small_up_grad,
        small_down_grad,
        wide_output,
        wide_grad,
        wide_gate_grad,
        wide_up_grad,
        wide_down_grad,
    )


def solution(mesh):
    grid = Mesh(mesh.devices.reshape(8, 4, 2, 4), WHOLE)
    rows = P(WHOLE, None)
    columns = P(None, WHOLE)
    return jax.shard_map(
        per_device,
        mesh=grid,
        in_specs=(
            rows, rows, rows, rows, columns, columns, rows, rows, rows, rows, columns, columns, rows,
        ),
        out_specs=(rows, rows, columns, columns, rows, rows, rows, columns, columns, rows),
        check_vma=False,
    )
```

```python
import jax
import jax.numpy as jnp
from jax import lax
from jax.experimental import pallas as pl
from jax.experimental.pallas import tpu as pltpu
from jax.sharding import Mesh, PartitionSpec as P

F32 = jnp.float32
BF16 = jnp.bfloat16
EXPERT = ("z", "y", "core")
WHOLE = ("z", "y", "core", "x")


def activation(gate_pre):
    sigma = jax.nn.sigmoid(gate_pre)
    return (gate_pre * sigma, sigma * (1.0 + gate_pre * (1.0 - sigma)))


def mm(a, b):
    return jnp.dot(a, b, preferred_element_type=F32)


def mm_nt(a, b):
    return jnp.einsum("rh,dh->rd", a, b, preferred_element_type=F32)


def mm_tn(a, b):
    return jnp.einsum("rd,rh->dh", a, b, preferred_element_type=F32)


def slot_rank(routing, experts, capacity):
    labels = jnp.arange(experts, dtype=jnp.int32)
    onehot = (routing[:, None] == labels[None, :]).astype(jnp.int32)
    earlier = jnp.cumsum(onehot, axis=0) - onehot
    return jnp.sum(earlier * onehot, axis=1)


def places(at, count):
    return (at[:, None] == jnp.arange(count, dtype=jnp.int32)[None, :]).astype(BF16)


def pair_perm(flip):
    perm = []
    for core in range(2):
        for x in range(4):
            mate = x ^ 1 if core ^ flip == 0 else 3 - x
            perm.append((core * 4 + x, core * 4 + mate))
    return perm


ROW_PAIR = pair_perm(0)
WEIGHT_PAIR = pair_perm(1)


def row_swap(v):
    return lax.ppermute(v, ("core", "x"), ROW_PAIR)


def weight_swap(v):
    return lax.ppermute(v, ("core", "x"), WEIGHT_PAIR)


def shift(v, axis, by):
    n = lax.axis_size(axis)
    return lax.ppermute(v, axis, [(i, (i + by) % n) for i in range(n)])


def mirror(v, axis, bit):
    return lax.ppermute(v, axis, [(i, i ^ bit) for i in range(lax.axis_size(axis))])


def gather_x(v):
    return jnp.concatenate([v, shift(v, "x", 1), shift(v, "x", -1), shift(v, "x", 2)], axis=0)


def gather_near(v):
    half = v.shape[0] // 2
    below, above = shift(v, "y", 1), shift(v, "y", -1)
    far_a, far_b = shift(below[:half], "y", 1), shift(above[half:], "y", -1)
    return [v, below, above, far_a, far_b]


def collect_far(own, sent):
    v = own + mirror(sent, "core", 1).astype(F32)
    half = v.shape[1] // 2
    far = v[3].astype(BF16)
    return v, shift(far[:half], "y", -1), shift(far[half:], "y", 1)


def collect_turn(v, from_a, from_b):
    below, above = v[1], v[2]
    half = below.shape[0] // 2
    from_a, from_b = from_a.astype(F32), from_b.astype(F32)
    below = jnp.concatenate([below[:half] + from_a, below[half:]], axis=0).astype(BF16)
    above = jnp.concatenate([above[:half], above[half:] + from_b], axis=0).astype(BF16)
    return below, above


def collect_near(v, below, above):
    return v[0] + shift(below, "y", -1).astype(F32) + shift(above, "y", 1).astype(F32)


def collect_x(v):
    rows = v.shape[0] // 4
    own, below, above, far = (v[i * rows : (i + 1) * rows] for i in range(4))
    v = own + shift(below.astype(BF16), "x", -1).astype(F32)
    v = v + shift(above.astype(BF16), "x", 1).astype(F32)
    return v + shift(far.astype(BF16), "x", 2).astype(F32)


def wide_kernel(*refs):
    pieces = refs[:10]
    place, gate, up, down, own_ref, sent_ref, dgate, dup, ddown = refs[11:20]
    rows, both, hidden, grads = refs[20:]
    width, units = gate.shape
    total, part = pieces[0].shape
    half = total // 2
    core, at_y = place[0], place[1]
    ys = [lax.rem(at_y + step, 4) for step in (0, 3, 1, 2)]
    for side in range(2):
        base = (core if side == 0 else 1 - core) * width
        spots = [pl.ds(pl.multiple_of(base + y * part, part), part) for y in ys]
        own, below, above, far_a, far_b = pieces[5 * side : 5 * side + 5]
        rows[:, spots[0]] = own[...]
        rows[:, spots[1]] = below[...]
        rows[:, spots[2]] = above[...]
        rows[:half, spots[3]] = far_a[...]
        rows[half:, spots[3]] = far_b[...]
    both[:, :units] = gate[...]
    both[:, units:] = up[...]
    chunk = 128

    @pl.loop(0, total // chunk)
    def _(i):
        here = pl.ds(pl.multiple_of(i * chunk, chunk), chunk)
        pre = mm(rows[here, :width], both[...])
        gate_pre, up_pre = pre[:, :units], pre[:, units:]
        active, slope = activation(gate_pre)
        hidden[here, :] = (active * up_pre).astype(BF16)
        back = nt(rows[here, width:], down[...])
        grads[here, :units] = (back * up_pre * slope).astype(BF16)
        grads[here, units:] = (back * active).astype(BF16)
        for j, y in enumerate(ys):
            spot = pl.ds(pl.multiple_of(y * part, part), part)
            out = mm(hidden[here, :], down[:, spot])
            grad = nt(grads[here, :], both[spot, :])
            own_ref[j, here, :] = jnp.where(core == 0, out, grad)
            sent_ref[j, here, :] = jnp.where(core == 0, grad, out).astype(BF16)

    block = 256

    @pl.loop(0, width // block)
    def _(i):
        here = pl.ds(pl.multiple_of(i * block, block), block)
        there = pl.ds(pl.multiple_of(width + i * block, block), block)
        term = tn(rows[:, here], grads[...])
        dgate[here, :] = term[:, :units].astype(BF16)
        dup[here, :] = term[:, units:].astype(BF16)
        ddown[:, here] = tn(hidden[...], rows[:, there]).astype(BF16)


def wide_compute(pieces, after, place, gate, up, down):
    width, units = gate.shape
    total, part = pieces[0].shape
    inside = pl.BlockSpec(memory_space=pltpu.VMEM)
    return pl.pallas_call(
        wide_kernel,
        out_shape=(
            jax.ShapeDtypeStruct((4, total, part), F32),
            jax.ShapeDtypeStruct((4, total, part), BF16),
            jax.ShapeDtypeStruct(gate.shape, BF16),
            jax.ShapeDtypeStruct(up.shape, BF16),
            jax.ShapeDtypeStruct(down.shape, BF16),
        ),
        in_specs=[inside] * 11 + [pl.BlockSpec(memory_space=pltpu.SMEM)] + [inside] * 3,
        out_specs=[inside] * 5,
        scratch_shapes=[
            pltpu.VMEM((total, 2 * width), BF16),
            pltpu.VMEM((width, 2 * units), BF16),
            pltpu.VMEM((total, units), BF16),
            pltpu.VMEM((total, 2 * units), BF16),
        ],
        compiler_params=pltpu.CompilerParams(vmem_limit_bytes=40 << 20),
        cost_estimate=pl.CostEstimate(
            flops=18 * total * width * units, bytes_accessed=16 << 20, transcendentals=total * units
        ),
    )(*pieces, after, place, gate, up, down)


def nt(a, b):
    return lax.dot_general(a, b, (((1,), (1,)), ((), ())), preferred_element_type=F32)


def tn(a, b):
    return lax.dot_general(a, b, (((0,), (0,)), ((), ())), preferred_element_type=F32)


def exchange(v):
    return lax.all_to_all(v, EXPERT, split_axis=0, concat_axis=0, tiled=True)


def per_device(
    note_tokens,
    note_route,
    note_prob,
    note_cotangent,
    small_gate,
    small_up,
    small_down,
    wide_tokens,
    wide_prob,
    wide_cotangent,
    wide_gate,
    wide_up,
    wide_down,
):
    width = note_tokens.shape[1]
    experts = lax.axis_size(EXPERT)
    capacity = max(2, 2 * note_tokens.shape[0] // experts)

    half = experts * capacity
    units = small_gate.shape[1]
    nz, ny, nc = (lax.axis_size(name) for name in EXPERT)
    members = wide_prob.shape[1]
    wide_rows = wide_tokens.shape[0]

    own_both = jnp.concatenate([small_gate, small_up], axis=1)

    part = 2 * width // (ny * nc)
    scaled = wide_prob.astype(F32)[:, :, None] * wide_cotangent.astype(F32)[:, None, :]
    pair = jnp.stack(
        [jnp.broadcast_to(wide_tokens[:, None, :], scaled.shape), scaled.astype(BF16)], axis=2
    )
    pair = pair.reshape(wide_rows, members, nc, ny, part).transpose(1, 3, 2, 0, 4)
    pair = jnp.broadcast_to(pair[:, None], (members, nz // members) + pair.shape[1:])
    near = exchange(pair.reshape(experts, wide_rows, part)).reshape(experts * wide_rows, part)

    routing = note_route[:, 0]
    rank = slot_rank(routing, experts, capacity)
    table = places(routing * capacity + rank, half)
    first = 2 * routing * capacity + rank
    row_table, cot_table = places(first, 2 * half), places(first + capacity, 2 * half)
    scaled_cot = (note_prob * note_cotangent.astype(F32)).astype(BF16)
    placed = mm_tn(
        jnp.concatenate([row_table, cot_table], axis=0),
        jnp.concatenate([note_tokens, scaled_cot], axis=0),
    ).astype(BF16)
    placed, near = lax.optimization_barrier((placed, near))
    arrived = exchange(placed.reshape(experts, 2 * capacity, width))

    near = gather_x(near)
    near, own_both, small_down = lax.optimization_barrier((near, own_both, small_down))
    mate_both = weight_swap(own_both)
    mate_down = weight_swap(small_down)
    wide_pieces = gather_near(near)
    *near_pieces, far_a, far_b = wide_pieces
    arrived, mate_both, mate_down, far_a, far_b = lax.optimization_barrier(
        (arrived, mate_both, mate_down, far_a, far_b)
    )
    wide_pieces = near_pieces + [far_a, far_b]
    wide_pieces = wide_pieces + [mirror(piece, "core", 1) for piece in wide_pieces]
    slot = jnp.arange(2 * half, dtype=jnp.int32)
    order = slot % half // capacity * 2 * capacity + slot // half * capacity + slot % capacity
    sorted_slots = mm(places(order, 2 * half), arrived.reshape(2 * half, width)).astype(BF16)
    own_rows, own_cots = sorted_slots[:half], sorted_slots[half:]
    rows = lax.optimization_barrier(jnp.concatenate([own_rows, row_swap(own_rows)], axis=0))
    mate_cots = row_swap(own_cots)

    place = jnp.stack([lax.axis_index("core"), lax.axis_index("y")]).astype(jnp.int32)
    wide_own, wide_sent, wide_gate_grad, wide_up_grad, wide_down_grad = wide_compute(
        wide_pieces, own_rows[:16, :128], place, wide_gate, wide_up, wide_down
    )


    boths, downs = (own_both, mate_both), (small_down, mate_down)
    blocks = (experts, capacity, width)
    hidden, terms, grads = [], [], []
    for w in range(2):
        pre = mm(rows, boths[w])
        gate_pre, up_pre = pre[:, :units], pre[:, units:]
        active, slope = activation(gate_pre)
        hidden.append((active * up_pre).astype(BF16))
        terms.append((up_pre, active, slope))

    def out_part(r):
        here = slice(r * half, (r + 1) * half)
        return mm(hidden[0][here], downs[0]) + mm(hidden[1][here], downs[1])

    sent_out, own_out, mate_cots = lax.optimization_barrier(
        (out_part(1).astype(BF16), out_part(0), mate_cots)
    )
    mate_out = row_swap(sent_out)
    wide_part, from_a, from_b = collect_far(wide_own, wide_sent)
    below, above = collect_turn(wide_part, from_a, from_b)
    mate_out, mate_cots, below, above = lax.optimization_barrier(
        (mate_out, mate_cots, below, above)
    )
    slot_out, mate_cots = lax.optimization_barrier(
        ((own_out + mate_out.astype(F32)).astype(BF16), mate_cots)
    )
    back_out = exchange(slot_out.reshape(blocks))
    cots = jnp.concatenate([own_cots, mate_cots], axis=0)
    for w in range(2):
        up_pre, active, slope = terms[w]
        grad_hidden = mm_nt(cots, downs[w])
        grads.append(
            jnp.concatenate(
                [
                    (grad_hidden * up_pre * slope).astype(BF16),
                    (grad_hidden * active).astype(BF16),
                ],
                axis=1,
            )
        )

    def grad_part(r):
        here = slice(r * half, (r + 1) * half)
        return mm_nt(grads[0][here], boths[0]) + mm_nt(grads[1][here], boths[1])

    mate_grad = row_swap(grad_part(1).astype(BF16))

    def both_term(w):
        return mm_tn(rows, grads[w])

    def down_term(w):
        return mm_tn(hidden[w], cots)

    side = part * wide_rows // capacity
    wide_part, both_sent = lax.optimization_barrier(
        (collect_near(wide_part, below, above), both_term(1).astype(BF16))
    )
    sums = collect_x(wide_part).astype(BF16).reshape(half, side)
    down_mate = weight_swap(down_term(1).astype(BF16))
    both_sent, down_mate, sums, own_grad, back_out = lax.optimization_barrier(
        (both_sent, down_mate, sums, grad_part(0), back_out)
    )
    slot_grad = (own_grad + mate_grad.astype(F32)).astype(BF16)
    back = jnp.concatenate([slot_grad, sums], axis=1).reshape(experts, capacity, -1)
    back = exchange(back).reshape(half, width + side)
    sums = back[:, width:].astype(F32).reshape(members, nz // members, ny, nc, wide_rows, part)
    sums = jnp.sum(sums, axis=1).transpose(0, 2, 3, 1, 4).reshape(members, nc, wide_rows, width)
    weights = wide_prob.astype(F32).T[:, :, None]
    wide_output = jnp.sum(sums[:, 0] * weights, axis=0).astype(BF16)
    wide_grad = jnp.sum(sums[:, 1], axis=0).astype(BF16)

    both_grad = (both_term(0) + weight_swap(both_sent).astype(F32)).astype(BF16)
    small_gate_grad, small_up_grad = both_grad[:, :units], both_grad[:, units:]
    small_down_grad = (down_term(0) + down_mate.astype(F32)).astype(BF16)

    note_output = (note_prob * mm(table, back_out.reshape(half, width))).astype(BF16)
    note_grad = mm(table, back[:, :width]).astype(BF16)
    return (
        note_output,
        note_grad,
        small_gate_grad,
        small_up_grad,
        small_down_grad,
        wide_output,
        wide_grad,
        wide_gate_grad,
        wide_up_grad,
        wide_down_grad,
    )


def solution(mesh):
    grid = Mesh(mesh.devices.reshape(8, 4, 2, 4), WHOLE)
    rows = P(WHOLE, None)
    columns = P(None, WHOLE)
    return jax.shard_map(
        per_device,
        mesh=grid,
        in_specs=(
            rows, rows, rows, rows, columns, columns, rows, rows, rows, rows, columns, columns, rows,
        ),
        out_specs=(rows, rows, columns, columns, rows, rows, rows, columns, columns, rows),
        check_vma=False,
    )
```
